32 devices in a mesh: ep: 32 (over z, y, x, core).
Axes of the slice: x: 2, y: 2, z: 4, core: 2. Of those that a mesh axis runs over, the one named last changes fastest.
Arguments:
- tokens: bfloat16 [2, 512, 3584], P(None, 'ep'), may hold values from -6 to 6
- expert_ids: int32 [2, 512, 8], P(None, 'ep'), may hold values from 0 to 31, all different within a row; in each aligned block of 16 rows (0 to 15, 16 to 31, ..., all dimensions but the last counted through in order) at most 8 rows name the same one
- combine_weights: float32 [2, 512, 8], P(None, 'ep'), may hold values from 0.05 to 0.5
- w_gate: bfloat16 [32, 3584, 1024], P('ep'), may hold values from -0.09375 to 0.09375
- w_up: bfloat16 [32, 3584, 1024], P('ep'), may hold values from -0.09375 to 0.09375
- w_down: bfloat16 [32, 1024, 3584], P('ep'), may hold values from -0.1875 to 0.1875
- shared_weights: bfloat16 [3, 3584, 4096], P(None, None, 'ep'), as said below
Outputs:
- moe_out: bfloat16 [2, 512, 3584], P(None, 'ep')
The draws below stay inside these ranges and needn't reach their ends.
Inputs may be any that keep to these rules, and one draw needn't show every extreme that they name: `expert_ids`: in each step the 16 rows of one device name any one expert at most 8 times; the 8 experts of a token differ. `shared_weights`: the array is 4 equal copies of one block of 1024 columns, laid end to end along the last dimension.
All inputs are finite; a program needn't handle non-finite values.
Results may differ from the reference program's by a relative error of at most 0.0055.
Values may be sent and summed in bfloat16 or wider, within the bound.
No kernel may reach another device: no remote copies, remote signals or barrier semaphores. Data moves between devices by JAX's collectives and lax.ppermute only.
A program may use at most 128 MiB of HBM per device.

```python
import math
import jax
import jax.numpy as jnp
import numpy as np
from jax import lax

D = 3584
FFE = 1024
FS = 1024
TOPK = 8
STEPS = 2
REQ_DEV = 16
TOKENS = 512
EXPERTS = 32
CAP = 8
SHARED_COLS = 4096
N_EP = 32


def draw_shared_weights(key, part):
    scale = D ** (-0.5)
    block = jnp.clip(jax.random.normal(key, (3, D, FS), jnp.float32), -6.0, 6.0) * scale
    copies = SHARED_COLS // FS
    return jnp.tile(block, (1, 1, copies)).astype(jnp.bfloat16)


def block_scale(rng, shape, pieces, smallest, top_value):
    gain = 1.0
    for dim, shards_of in pieces:
        draws = jax.random.uniform(jax.random.fold_in(jax.random.fold_in(rng, 6), dim), (shards_of,), jnp.float32, smallest / len(pieces), top_value / len(pieces))
        gain = gain * jnp.repeat(jnp.exp(draws), shape[dim] // shards_of).reshape((-1,) + (1,) * (len(shape) - 1 - dim))
    return gain


def assign_block(key, own, number, rows, number_of, top, most, skew):
    order = jax.random.permutation(key, number_of)
    heavy_load, ordinary = shares(number_of, rows * top, most, skew, True), shares(number_of, rows * top, most, skew, False)
    places = jnp.arange(number_of)

    def named(lengths, offset_by):
        used = int((lengths > 0).sum())
        fixed = max(1, used // 4)
        moved = fixed + (places - fixed + offset_by * (used - fixed)) % max(1, number_of - fixed)
        return jnp.zeros((number_of,), jnp.int32).at[order[jnp.where(places < fixed, places, moved)]].set(jnp.asarray(lengths, jnp.int32))

    lengths = jnp.where(number % 4 == 0, named(heavy_load, number // 4), named(ordinary, number - number // 4 - 1))
    mixed = jax.random.permutation(jax.random.fold_in(own, 3), number_of)
    giver, sink = mixed[0:number_of // 2 * 2:2], mixed[1:number_of // 2 * 2:2]
    room = jnp.minimum(lengths[giver] - 1, most - lengths[sink]) // 2
    room = jnp.where((giver == order[0]) | (sink == order[0]) | (lengths[sink] == 0), 0, jnp.maximum(room, 0))
    moved = jax.random.randint(jax.random.fold_in(own, 4), (number_of // 2,), 0, 1 << 20) % (room + 1)
    lengths = lengths.at[giver].add(-moved).at[sink].add(moved)
    labels = jnp.searchsorted(jnp.cumsum(lengths), jnp.arange(rows * top), side="right").astype(jnp.int32)
    table = labels.reshape(top, rows).T
    table = table[jax.random.permutation(jax.random.fold_in(own, 1), rows)]
    offset_by = jax.random.randint(jax.random.fold_in(own, 2), (rows, 1), 0, top)
    return jnp.take_along_axis(table, (jnp.arange(top)[None, :] + offset_by) % top, axis=1)


def shares(amount, total, reach, slope, full):
    portions = [(1 << 20) // math.isqrt(rank ** slope) + 1 for rank in range(1, amount + 1)]
    largest = reach if full else min(reach, max(-(-total // amount), total * portions[0] // sum(portions)))
    least = 1 if total - largest >= amount - 1 else 0
    holding, spare = [largest] + [least] * (amount - 1), total - largest - least * (amount - 1)
    while spare > 0:
        movable = [i for i in range(1, amount) if holding[i] < largest] or [i for i in range(1, amount) if holding[i] < reach]
        mass, left = sum([portions[i] for i in movable]), spare
        for i in movable:
            extra = min(reach - holding[i], max(1, left * portions[i] // mass), spare)
            holding[i] = holding[i] + extra
            spare = spare - extra
    return np.array(holding)


def bell_draw(own_key, dims, scale, limit, pieces=(), kind=jnp.bfloat16):
    entries = jax.random.normal(own_key, dims, jnp.float32) * scale
    if len(pieces) > 0:
        entries = block_scale(own_key, dims, pieces, -0.22, 0.18) * entries
    return jnp.clip(entries, min=-limit, max=limit).astype(kind)


def setup_inputs(seed: int = 0) -> dict:
    arg_keys = jax.random.split(jax.random.key(seed), 8)
    tokens = bell_draw(arg_keys[0], (STEPS, TOKENS, D), 1.0, 6.0, ((1, 32),))
    expert_ids_keys = jax.random.split(jax.random.fold_in(arg_keys[1], 1), STEPS * TOKENS // REQ_DEV)
    expert_ids_turns = jax.random.permutation(jax.random.fold_in(arg_keys[1], 3), STEPS * TOKENS // REQ_DEV)
    expert_ids = jax.vmap(lambda own, number: assign_block(jax.random.fold_in(arg_keys[1], 2), own, number, REQ_DEV, EXPERTS, TOPK, CAP, 2))(expert_ids_keys, expert_ids_turns).reshape((STEPS, TOKENS, TOPK))
    combine_weights = jnp.clip(jnp.exp(math.log(0.5) - 2.3025851 * jax.random.uniform(arg_keys[2], (STEPS, TOKENS, TOPK), jnp.float32) ** block_scale(arg_keys[2], (STEPS, TOKENS, TOPK), ((1, 32),), -0.2, 0.2)), 0.05, 0.5)
    w_gate = bell_draw(arg_keys[3], (EXPERTS, D, FFE), D ** -0.5, 0.09375, ((0, 32),))
    w_up = bell_draw(arg_keys[4], (EXPERTS, D, FFE), D ** -0.5, 0.09375, ((0, 32),))
    w_down = bell_draw(arg_keys[5], (EXPERTS, FFE, D), FFE ** -0.5, 0.1875, ((0, 32),))
    shared_weights = draw_shared_weights(jax.random.fold_in(arg_keys[7], 71), 0)
    return {"tokens": tokens, "expert_ids": expert_ids, "combine_weights": combine_weights, "w_gate": w_gate, "w_up": w_up, "w_down": w_down, "shared_weights": shared_weights}


def expert_rows(token_rows, gate_mat, up_mat, down_mat):
    gate_val = jnp.dot(token_rows, gate_mat, preferred_element_type=jnp.float32)
    up_val = jnp.dot(token_rows, up_mat, preferred_element_type=jnp.float32)
    hidden = (jax.nn.silu(gate_val) * up_val).astype(jnp.bfloat16)
    return jnp.dot(hidden, down_mat, preferred_element_type=jnp.float32).astype(jnp.bfloat16)


def reference(tokens, expert_ids, combine_weights, w_gate, w_up, w_down, shared_weights):
    pairs = REQ_DEV * TOPK
    flat_ids = expert_ids.reshape(STEPS, N_EP, pairs)
    onehot = (flat_ids[..., None] == jnp.arange(EXPERTS, dtype=jnp.int32)).astype(jnp.int32)
    slot_index = jnp.sum((jnp.cumsum(onehot, axis=2) - onehot) * onehot, axis=3).astype(jnp.int32)
    local_tok = jnp.broadcast_to(jnp.arange(pairs, dtype=jnp.int32) // TOPK, (STEPS, N_EP, pairs))
    step_idx = jnp.broadcast_to(jnp.arange(STEPS, dtype=jnp.int32)[:, None, None], (STEPS, N_EP, pairs))
    block_idx = jnp.broadcast_to(jnp.arange(N_EP, dtype=jnp.int32)[None, :, None], (STEPS, N_EP, pairs))
    source = jnp.zeros((STEPS, N_EP, EXPERTS, CAP), jnp.int32).at[step_idx, block_idx, flat_ids, slot_index].set(local_tok)
    weight_tab = jnp.zeros((STEPS, N_EP, EXPERTS, CAP), jnp.float32).at[step_idx, block_idx, flat_ids, slot_index].set(
        combine_weights.reshape(STEPS, N_EP, pairs).astype(jnp.float32))
    grid = tokens.reshape(STEPS, N_EP, REQ_DEV, D)
    step_b = jnp.broadcast_to(jnp.arange(STEPS, dtype=jnp.int32)[:, None, None], (STEPS, N_EP, CAP))
    block_b = jnp.broadcast_to(jnp.arange(N_EP, dtype=jnp.int32)[None, :, None], (STEPS, N_EP, CAP))

    def one_expert(totals, inputs):
        gate_mat, up_mat, down_mat, src, wts = inputs
        chosen = jnp.take_along_axis(grid, src[..., None], axis=2)
        outputs = expert_rows(chosen.reshape(-1, D), gate_mat, up_mat, down_mat).reshape(STEPS, N_EP, CAP, D)
        weighted = outputs.astype(jnp.float32) * wts[..., None]
        return totals.at[step_b, block_b, src].add(weighted), None

    start = jnp.zeros((STEPS, N_EP, REQ_DEV, D), jnp.float32)
    routed, _ = lax.scan(one_expert, start, (w_gate, w_up, w_down,
                                             jnp.transpose(source, (2, 0, 1, 3)),
                                             jnp.transpose(weight_tab, (2, 0, 1, 3))))
    block_weights = shared_weights[:, :, :FS]
    flat_rows = tokens.reshape(-1, D)
    gate_val = jnp.dot(flat_rows, block_weights[0], preferred_element_type=jnp.float32)
    up_val = jnp.dot(flat_rows, block_weights[1], preferred_element_type=jnp.float32)
    shared_hidden = (jax.nn.silu(gate_val) * up_val).astype(jnp.bfloat16)
    shared_out = jnp.dot(shared_hidden, block_weights[2].T, preferred_element_type=jnp.float32)
    total = shared_out.reshape(STEPS, N_EP, REQ_DEV, D) + routed
    return total.reshape(STEPS, TOKENS, D).astype(jnp.bfloat16)
```

```python
import functools

import jax
import jax.numpy as jnp
from jax import lax
from jax.experimental import pallas as pl
from jax.experimental.pallas import tpu as pltpu
from jax.sharding import PartitionSpec as P

AXIS = "ep"
GROUP = 8


def swap(block, mask_even, mask_odd):
    count = lax.axis_size(AXIS)
    route = [(i, i ^ (mask_odd if i & 1 else mask_even)) for i in range(count)]
    return lax.ppermute(block, AXIS, route)


def first_hop(block):
    return swap(block, 2, 4)


def second_hop(block):
    return swap(block, 4, 2)


def across(block, k):
    return swap(block, GROUP * k, GROUP * k)


def other_core(block):
    return swap(block, 1, 1)


def routing_columns(expert_ids, combine_weights, experts):
    step_count, row_count, _ = expert_ids.shape
    named = expert_ids[..., None] == jnp.arange(experts, dtype=jnp.int32)
    present = jnp.any(named, axis=2)
    weight = jnp.sum(jnp.where(named, combine_weights[..., None], 0.0), axis=2)
    earlier = (jnp.arange(row_count)[:, None] > jnp.arange(row_count)[None, :])[None, :, :, None]
    before = jnp.sum(jnp.where(earlier & present[:, None], 1.0, 0.0), axis=2)
    slot = jnp.where(present, before, -1.0)
    high = lax.reduce_precision(weight, 8, 7)
    low = weight - high
    columns = jnp.concatenate([slot, high, low], axis=2).astype(jnp.bfloat16)
    pad = -columns.shape[2] % 128
    return jnp.pad(columns, ((0, 0), (0, 0), (0, pad)))


def ffn_kernel(parts, me_ref, x_ref, gate_ref, up_ref, down_ref, out_ref, hidden):
    first_parts, width, experts = parts
    step = pl.program_id(0)
    tile = gate_ref.shape[1]

    @pl.when(step < first_parts)
    def _():
        rows = x_ref[:, :width]
        gate_val = jnp.dot(rows, gate_ref[...], preferred_element_type=jnp.float32)
        up_val = jnp.dot(rows, up_ref[...], preferred_element_type=jnp.float32)
        value = gate_val / (1.0 + jnp.exp(-gate_val)) * up_val
        hidden[:, pl.ds(pl.multiple_of(step * tile, tile), tile)] = value.astype(jnp.bfloat16)

    @pl.when(step >= first_parts)
    def _():
        columns = x_ref[:, width:].astype(jnp.float32)
        lane = lax.broadcasted_iota(jnp.int32, columns.shape, 1)
        mine = (lane == me_ref[0] + experts) | (lane == me_ref[0] + 2 * experts)
        weight = jnp.sum(jnp.where(mine, columns, 0.0), axis=1, keepdims=True)
        value = jnp.dot(hidden[...], down_ref[...], preferred_element_type=jnp.float32)
        out_ref[...] = (value * weight).astype(jnp.bfloat16)


def ffn(x, me, w_gate, w_up, w_down, experts):
    rows, full = x.shape
    _, width, units = w_gate.shape
    tile_j, tile_n = 256, 512
    first_parts, second_parts = units // tile_j, width // tile_n
    grid_spec = pltpu.PrefetchScalarGridSpec(
        num_scalar_prefetch=1,
        grid=(first_parts + second_parts,),
        in_specs=[
            pl.BlockSpec((rows, full), lambda i, m: (0, 0)),
            pl.BlockSpec((None, width, tile_j), lambda i, m: (0, 0, jnp.minimum(i, first_parts - 1))),
            pl.BlockSpec((None, width, tile_j), lambda i, m: (0, 0, jnp.minimum(i, first_parts - 1))),
            pl.BlockSpec((None, units, tile_n), lambda i, m: (0, 0, jnp.maximum(i - first_parts, 0))),
        ],
        out_specs=pl.BlockSpec((rows, tile_n), lambda i, m: (0, jnp.maximum(i - first_parts, 0))),
        scratch_shapes=[pltpu.VMEM((rows, units), jnp.bfloat16)],
    )
    return pl.pallas_call(
        functools.partial(ffn_kernel, (first_parts, width, experts)),
        grid_spec=grid_spec,
        out_shape=jax.ShapeDtypeStruct((rows, width), jnp.bfloat16),
        compiler_params=pltpu.CompilerParams(vmem_limit_bytes=32 * 1024 * 1024),
        cost_estimate=pl.CostEstimate(
            flops=6 * rows * width * units, bytes_accessed=6 * width * units, transcendentals=rows * units
        ),
        name="expert_ffn",
    )(me, x, w_gate, w_up, w_down)


def placing(columns, expert, row_count, capacity):
    rows = columns.shape[0]
    slots = rows // row_count * capacity
    slot = lax.dynamic_slice_in_dim(columns, expert, 1, axis=1).astype(jnp.int32)
    base = (jnp.arange(rows, dtype=jnp.int32) // row_count * capacity)[:, None]
    target = jnp.where(slot >= 0, base + slot, -1)
    return (target == jnp.arange(slots, dtype=jnp.int32)[None, :]).astype(jnp.bfloat16)


def shards(tokens, expert_ids, combine_weights, w_gate, w_up, w_down, shared_weights):
    step_count, row_count, width = tokens.shape
    top_count = expert_ids.shape[2]
    devices = lax.axis_size(AXIS)
    experts = w_gate.shape[0] * devices
    capacity = max(2, row_count * top_count * 2 // experts)
    planes = devices // GROUP
    me = lax.axis_index(AXIS)
    block = step_count * row_count

    columns = routing_columns(expert_ids, combine_weights, experts)
    own = jnp.concatenate([tokens, columns], axis=2).reshape(block, -1)

    shared_other = other_core(shared_weights)

    def spread(rows):
        rows = jnp.concatenate([rows, first_hop(rows)], axis=0)
        return jnp.concatenate([rows, second_hop(rows)], axis=0)

    gathered = [None] * planes
    far = [own] + [across(own, k) for k in range(1, planes)]
    gathered0 = spread(own)
    gathered1 = spread(far[1])
    rest = jnp.stack(far[2:], axis=0).reshape(-1, own.shape[1])
    gathered_rest = spread(rest)

    def experts_of(rows):
        place = jnp.concatenate(
            [placing(rows[:, width:], me, row_count, capacity), placing(rows[:, width:], me ^ 1, row_count, capacity)],
            axis=1,
        )
        chosen = lax.dot_general(
            place, rows, (((0,), (0,)), ((), ())), preferred_element_type=jnp.float32
        ).astype(jnp.bfloat16)
        half = chosen.shape[0] // 2
        received = other_core(chosen[half:])
        result = ffn(
            jnp.concatenate([chosen[:half], received], axis=0), me[None], w_gate, w_up, w_down, experts
        )
        returned = other_core(result[half:])
        return jnp.dot(
            place, jnp.concatenate([result[:half], returned], axis=0), preferred_element_type=jnp.float32
        )

    def shared_expert(rows):
        hidden = []
        for part in (shared_weights, shared_other):
            gate_val = jnp.dot(rows, part[0], preferred_element_type=jnp.float32)
            up_val = jnp.dot(rows, part[1], preferred_element_type=jnp.float32)
            hidden.append((jax.nn.silu(gate_val) * up_val).astype(jnp.bfloat16))
        return sum(
            lax.dot_general(h, part[2], (((1,), (1,)), ((), ())), preferred_element_type=jnp.float32)
            for h, part in zip(hidden, (shared_weights, shared_other))
        )

    def collect(partial):
        half = partial.shape[0] // 2
        partial = partial[:half] + second_hop(partial[half:].astype(jnp.bfloat16)).astype(jnp.float32)
        half = half // 2
        return partial[:half] + first_hop(partial[half:].astype(jnp.bfloat16)).astype(jnp.float32)

    first = experts_of(jnp.concatenate([gathered0, gathered1], axis=0))
    partial0 = first[: GROUP // 2 * block] + shared_expert(gathered0[:, :width])
    partial1 = first[GROUP // 2 * block :]
    partial_rest = experts_of(gathered_rest)

    total1 = across(collect(partial1).astype(jnp.bfloat16), 1)
    summed_rest = collect(partial_rest).astype(jnp.bfloat16)
    parts = [total1] + [
        across(summed_rest[(k - 2) * block : (k - 1) * block], k) for k in range(2, planes)
    ]
    total = collect(partial0)
    for part in parts:
        total = total + part.astype(jnp.float32)
    return total.astype(jnp.bfloat16).reshape(step_count, row_count, width)


def solution(mesh):
    placed = (
        P(None, AXIS, None),
        P(None, AXIS, None),
        P(None, AXIS, None),
        P(AXIS, None, None),
        P(AXIS, None, None),
        P(AXIS, None, None),
        P(None, None, AXIS),
    )
    return jax.shard_map(
        shards, mesh=mesh, in_specs=placed, out_specs=P(None, AXIS, None), check_vma=False
    )
```

```python
import functools

import jax
import jax.numpy as jnp
from jax import lax
from jax.experimental import pallas as pl
from jax.experimental.pallas import tpu as pltpu
from jax.sharding import PartitionSpec as P

AXIS = "ep"
GROUP = 8
WHOLE = pl.BlockSpec(memory_space=pltpu.VMEM)
ANYWHERE = pl.BlockSpec(memory_space=pl.ANY)
SCALAR = pl.BlockSpec(memory_space=pltpu.SMEM)
F32, BF16 = jnp.float32, jnp.bfloat16


def swap(block, mask_even, mask_odd):
    count = lax.axis_size(AXIS)
    route = [(i, i ^ (mask_odd if i & 1 else mask_even)) for i in range(count)]
    return lax.ppermute(block, AXIS, route)


def first_hop(block):
    return swap(block, 2, 4)


def second_hop(block):
    return swap(block, 4, 2)


def across(block, k):
    return swap(block, GROUP * k, GROUP * k)


def other_core(block):
    return swap(block, 1, 1)


def far_off(array):
    return pltpu.with_memory_space_constraint(array, pltpu.HBM)


def near(array):
    return pltpu.with_memory_space_constraint(array, pltpu.VMEM)


class Line:
    def __init__(self):
        self.last = []

    def __call__(self, kernel, name, outs, scalars, arrays, scratch=(), alias=None, stored=(), inside=True, mib=8):
        count, waits = len(scalars) + len(arrays) + len(stored), len(self.last)

        def body(*refs):
            kernel(*refs[:count], *refs[count + waits :])

        result = pl.pallas_call(
            body,
            in_specs=[SCALAR] * len(scalars) + [WHOLE] * len(arrays) + [ANYWHERE] * (len(stored) + waits),
            out_specs=[WHOLE] * len(outs),
            out_shape=[(pltpu.VMEM if inside else jax.ShapeDtypeStruct)(shape, dtype) for shape, dtype in outs],
            scratch_shapes=scratch,
            input_output_aliases=alias or {},
            compiler_params=pltpu.CompilerParams(vmem_limit_bytes=mib * 1024 * 1024),
            cost_estimate=pl.CostEstimate(flops=1, bytes_accessed=1, transcendentals=0),
            name=name,
        )(*scalars, *[near(a) for a in arrays], *[far_off(a) for a in stored], *self.last)
        self.last = [result[0]]
        return result


def own_kernel(sizes, me_ref, choice_ref, tokens_ref, own_ref, held, sems):
    width, row_count, experts = sizes
    rows, full = own_ref.shape
    copy = pltpu.make_async_copy(tokens_ref, held, sems.at[0])
    copy.start()
    choice = choice_ref[...]
    top_count = choice.shape[1] // 2
    ids, weights = choice[:, :top_count].astype(jnp.int32), choice[:, top_count:]
    lane = lax.broadcasted_iota(jnp.int32, (rows, full - width), 1)
    present = jnp.zeros((rows, full - width), F32)
    weight = jnp.zeros((rows, full - width), F32)
    for k in range(ids.shape[1]):
        named = lax.rem(lane, experts) == ids[:, k : k + 1]
        present = jnp.where(named, 1.0, present)
        weight = jnp.where(named, weights[:, k : k + 1], weight)
    row = lax.broadcasted_iota(jnp.int32, (rows, rows), 0)
    column = lax.broadcasted_iota(jnp.int32, (rows, rows), 1)
    earlier = (row > column) & (row // row_count == column // row_count)
    before = jnp.dot(jnp.where(earlier, 1.0, 0.0).astype(BF16), present.astype(BF16), preferred_element_type=F32)
    slot = jnp.where(present > 0.0, before, -1.0)
    high = weight.astype(BF16).astype(F32)
    value = jnp.where(lane < experts, slot, jnp.where(lane < 2 * experts, high, weight - high))
    own_ref[:, width:] = value.astype(BF16)
    copy.wait()
    for s in range(held.shape[0]):
        own_ref[s * row_count : (s + 1) * row_count, :width] = held[s]


def load_kernel(weights_ref, held_ref, sems):
    pieces = sems.shape[0]
    rows = weights_ref.shape[1] // pieces
    copies = []
    for i in range(pieces):
        part = (slice(None), pl.ds(i * rows, rows))
        copies.append(pltpu.make_async_copy(weights_ref.at[part], held_ref.at[part], sems.at[i]))
    for copy in copies:
        copy.start()
    for copy in copies:
        copy.wait()


def pick(columns, lane_index):
    lane = lax.broadcasted_iota(jnp.int32, columns.shape, 1)
    return jnp.sum(jnp.where(lane == lane_index, columns, 0.0), axis=1, keepdims=True)


def placing(columns, expert, first_row, slots, row_count, capacity):
    rows = columns.shape[0]
    slot = pick(columns, expert).astype(jnp.int32)
    row = lax.broadcasted_iota(jnp.int32, (rows, 1), 0) + first_row
    target = jnp.where(slot >= 0, row // row_count * capacity + slot, -1)
    lane = lax.broadcasted_iota(jnp.int32, (rows, slots), 1)
    return jnp.where(lane == target, 1.0, 0.0).astype(BF16)


def gate_kernel(given_ref, out_ref):
    pass


def pack_kernel(*refs):
    *parts, out = refs
    start = 0
    for part in parts:
        rows = part.shape[0]
        out[start : start + rows, :] = part[...]
        start += rows


def dispatch_kernel(sizes, me_ref, a_ref, b_ref, own_ref, other_ref):
    width, row_count, capacity = sizes
    slots = own_ref.shape[0]
    rows = a_ref.shape[0]
    for out, expert in ((own_ref, me_ref[0]), (other_ref, me_ref[0] ^ 1)):
        place = [
            placing(ref[:, width:].astype(F32), expert, first, slots, row_count, capacity)
            for ref, first in ((a_ref, 0), (b_ref, rows))
        ]
        place = jnp.concatenate(place, axis=0).T
        for ref, first in ((a_ref, 0), (b_ref, rows)):
            half = slots // 2
            lower = first // row_count * capacity
            out[lower : lower + half, :] = jnp.dot(
                place[lower : lower + half, first : first + rows], ref[...], preferred_element_type=F32
            ).astype(BF16)


def expert_kernel(experts, me_ref, own_ref, got_ref, gate_ref, up_ref, down_ref, mine_ref, sent_ref, rows_ref, hidden):
    _, width, units = gate_ref.shape
    slots = own_ref.shape[0]
    rows_ref[:slots, :] = own_ref[...]
    rows_ref[slots:, :] = got_ref[...]
    columns = rows_ref[:, width:].astype(F32)
    weight = pick(columns, me_ref[0] + experts) + pick(columns, me_ref[0] + 2 * experts)
    tile = 256
    for j in range(0, units, tile):
        rows = rows_ref[:, :width]
        gate_val = jnp.dot(rows, gate_ref[0, :, j : j + tile], preferred_element_type=F32)
        up_val = jnp.dot(rows, up_ref[0, :, j : j + tile], preferred_element_type=F32)
        hidden[:, j : j + tile] = (gate_val / (1.0 + jnp.exp(-gate_val)) * up_val).astype(BF16)
    tile = 512
    for n in range(0, width, tile):
        value = jnp.dot(hidden[...], down_ref[0, :, n : n + tile], preferred_element_type=F32)
        value = (value * weight).astype(BF16)
        mine_ref[:, n : n + tile] = value[:slots]
        sent_ref[:, n : n + tile] = value[slots:]


def shared_kernel(a_ref, b_ref, first_ref, second_ref, out_ref):
    width = first_ref.shape[1]
    rows = a_ref.shape[0]
    for half, ref in enumerate((a_ref, b_ref)):
        hidden = []
        for part in (first_ref, second_ref):
            gate_val = jnp.dot(ref[:, :width], part[0], preferred_element_type=F32)
            up_val = jnp.dot(ref[:, :width], part[1], preferred_element_type=F32)
            hidden.append((gate_val / (1.0 + jnp.exp(-gate_val)) * up_val).astype(BF16))
        tile = 512
        for n in range(0, width, tile):
            value = 0.0
            for h, part in zip(hidden, (first_ref, second_ref)):
                value += lax.dot_general(
                    h, part[2, n : n + tile, :], (((1,), (1,)), ((), ())), preferred_element_type=F32
                )
            out_ref[half * rows : (half + 1) * rows, n : n + tile] = value


def combine_kernel(sizes, me_ref, a_ref, b_ref, mine_ref, back_ref, *refs):
    width, row_count, capacity = sizes
    *extra, keep_ref, send_ref = refs
    slots = mine_ref.shape[0]
    rows = a_ref.shape[0]
    half = slots // 2
    for ref, out, first in ((a_ref, keep_ref, 0), (b_ref, send_ref, rows)):
        columns = ref[:, width:].astype(F32)
        lower = first // row_count * capacity
        here = [
            placing(columns, e, 0, half, row_count, capacity) for e in (me_ref[0], me_ref[0] ^ 1)
        ]
        tile = 512
        for n in range(0, width, tile):
            value = sum(
                jnp.dot(p, part[lower : lower + half, n : n + tile], preferred_element_type=F32)
                for p, part in zip(here, (mine_ref, back_ref))
            )
            for part in extra:
                value += part[first : first + rows, n : n + tile]
            out[:, n : n + tile] = value.astype(out.dtype)


def middle_kernel(keep_ref, got_ref, *refs):
    *early, rest_ref, send_ref = refs
    half = rest_ref.shape[0]
    rest = keep_ref[:half, :] + got_ref[:half, :].astype(F32)
    for part in early:
        rest = rest + part[...].astype(F32)
    rest_ref[...] = rest
    send_ref[...] = (keep_ref[half:, :] + got_ref[half:, :].astype(F32)).astype(BF16)


def sum_kernel(*refs):
    *parts, out = refs
    total = parts[0][...]
    for part in parts[1:]:
        total = total + part[...].astype(F32)
    out[...] = total.astype(BF16).reshape(out.shape)


def shards(tokens, expert_ids, combine_weights, w_gate, w_up, w_down, shared_weights):
    step_count, row_count, width = tokens.shape
    top_count = expert_ids.shape[2]
    devices = lax.axis_size(AXIS)
    experts = w_gate.shape[0] * devices
    capacity = max(2, row_count * top_count * 2 // experts)
    planes = devices // GROUP
    units = w_gate.shape[2]
    index = lax.axis_index(AXIS)[None].astype(jnp.int32)
    block = step_count * row_count
    rows = GROUP // 2 * block
    slots = rows // row_count * capacity
    full = width + (3 * experts + 127) // 128 * 128
    sizes = (width, row_count, capacity)
    line = Line()

    choice = jnp.concatenate([expert_ids.astype(F32), combine_weights], axis=2)
    own, = line(
        functools.partial(own_kernel, (width, row_count, experts)),
        "own",
        [((block, full), BF16)],
        [index],
        [choice.reshape(block, 2 * top_count)],
        stored=[tokens],
        scratch=[pltpu.VMEM(tokens.shape, BF16), pltpu.SemaphoreType.DMA((1,))],
    )
    shared_other = other_core(shared_weights)
    far = {0: own, 1: across(own, 1), 2: across(own, 2)}
    held = {}
    hop, both, wide, leaving, chosen, mine, back, part, last, arrived = ({} for _ in range(10))

    def load(name, weights):
        held[name], = line(
            load_kernel,
            "load",
            [(weights.shape, BF16)],
            [],
            [],
            stored=[weights],
            scratch=[pltpu.SemaphoreType.DMA((4,))],
        )

    def enter(k):
        if k > 0:
            far[k], = line(gate_kernel, "enter", [((block, full), BF16)], [], [far[k]], alias={0: 0})
        if k >= 2 and k + 1 < planes:
            if k & 1 == 0:
                far[k + 1] = across(far[k], 1)
        hop[k] = first_hop(far[k])

    def pack(k):
        both[k], = line(pack_kernel, "pack", [((2 * block, full), BF16)], [], [far[k], hop[k]])
        wide[k] = second_hop(both[k])

    def dispatch(k):
        chosen[k], out = line(
            functools.partial(dispatch_kernel, sizes), "dispatch", [((slots, full), BF16)] * 2, [index], [both[k], wide[k]]
        )
        leaving[k] = other_core(out)

    def expert(k):
        mine[k], out = line(
            functools.partial(expert_kernel, experts),
            "expert",
            [((slots, width), BF16)] * 2,
            [index],
            [chosen[k], leaving[k], held["gate"], held["up"], held["down"]],
            scratch=[pltpu.VMEM((2 * slots, full), BF16), pltpu.VMEM((2 * slots, units), BF16)],
        )
        back[k] = other_core(out)

    def shared():
        part["shared"], = line(
            shared_kernel, "shared", [((rows, width), F32)], [], [both[0], wide[0], shared_weights, shared_other]
        )

    def combine(k):
        extra = [part["shared"]] if k == 0 else []
        keep, send = line(
            functools.partial(combine_kernel, sizes),
            "combine",
            [((2 * block, width), F32), ((2 * block, width), BF16)],
            [index],
            [both[k], wide[k], mine[k], back[k], *extra],
        )
        part[k] = (keep, second_hop(send))

    def middle(k, early=()):
        keep, send = line(
            middle_kernel,
            "middle",
            [((block, width), F32), ((block, width), BF16)],
            [],
            [*part[k], *[arrived.pop(j) for j in early]],
        )
        last[k] = (keep, first_hop(send))

    def leave(k):
        out, = line(sum_kernel, "leave", [((block, width), BF16)], [], list(last[k]))
        arrived[k] = across(out, k)

    def final():
        out, = line(
            sum_kernel,
            "final",
            [((step_count, row_count, width), BF16)],
            [],
            [*last[0], *[arrived[k] for k in arrived]],
            inside=False,
        )
        return out

    enter(0)
    pack(0)
    load("gate", w_gate)
    enter(1)
    if planes == 4:
        enter(2)
        dispatch(0)
        pack(1)
        load("up", w_up)
        pack(2)
        enter(3)
        load("down", w_down)
        dispatch(1)
        pack(3)
        dispatch(2)
        expert(1)
        expert(2)
        combine(2)
        dispatch(3)
        combine(1)
        expert(3)
        middle(2)
        combine(3)
        middle(1)
        leave(2)
        expert(0)
        shared()
        middle(3)
        leave(1)
        combine(0)
        leave(3)
        middle(0, early=(2, 1))
    else:
        load("gate", w_gate)
        load("up", w_up)
        load("down", w_down)
        pack(1)
        for k in range(2, planes):
            if k not in far:
                far[k] = across(own, k)
            enter(k)
            pack(k)
        for k in range(planes):
            dispatch(k)
            expert(k)
        shared()
        for k in reversed(range(planes)):
            combine(k)
            middle(k)
            if k > 0:
                leave(k)
    return final()


def solution(mesh):
    placed = (
        P(None, AXIS, None),
        P(None, AXIS, None),
        P(None, AXIS, None),
        P(AXIS, None, None),
        P(AXIS, None, None),
        P(AXIS, None, None),
        P(None, None, AXIS),
    )
    return jax.shard_map(
        shards, mesh=mesh, in_specs=placed, out_specs=P(None, AXIS, None), check_vma=False
    )
```

```python
import functools

import jax
import jax.numpy as jnp
from jax import lax
from jax.experimental import pallas as pl
from jax.experimental.pallas import tpu as pltpu
from jax.sharding import PartitionSpec as P

AXIS = "ep"
GROUP = 8
WHOLE = pl.BlockSpec(memory_space=pltpu.VMEM)
ANYWHERE = pl.BlockSpec(memory_space=pl.ANY)
SCALAR = pl.BlockSpec(memory_space=pltpu.SMEM)
F32, BF16 = jnp.float32, jnp.bfloat16


def swap(block, mask_even, mask_odd):
    count = lax.axis_size(AXIS)
    route = [(i, i ^ (mask_odd if i & 1 else mask_even)) for i in range(count)]
    return lax.ppermute(block, AXIS, route)


def first_hop(block):
    return swap(block, 2, 4)


def second_hop(block):
    return swap(block, 4, 2)


def across(block, k):
    return swap(block, GROUP * k, GROUP * k)


def other_core(block):
    return swap(block, 1, 1)


def far_off(array):
    return pltpu.with_memory_space_constraint(array, pltpu.HBM)


def near(array):
    return pltpu.with_memory_space_constraint(array, pltpu.VMEM)


ORDER = (
    "E0", "K0", "L0", "E1", "E2", "K1", "S0", "K2", "E3", "D0:w1", "K3:w0", "D1:w0", "D2", "X1",
    "D3", "X3", "X2", "C0", "C1", "X0", "M0", "C2:w2", "V0:w2:h2", "M1:w0", "C3:h0", "M2", "V1",
    "M3:g0", "V2:w3", "V3:w3",
)
GATHER_GROUPS = ((0,), (1,), (2,), (3,))
REDUCE_GROUPS = ((3,), (2,), (1,), (0,))


def any_groups(planes):
    gather = tuple((k,) for k in range(planes))
    reduce = tuple((k,) for k in reversed(range(planes)))
    steps = ["E0", "K0", "L0"]
    for k in range(1, planes):
        steps += [f"E{k}", f"K{k}"]
    steps += ["S0"]
    for i, (k,) in enumerate(reduce):
        steps += [f"D{k}", f"X{k}", f"C{i}", f"M{i}", f"V{i}"]
    return gather, reduce, steps


class Line:
    def __init__(self):
        self.last = []
        self.also = []

    def __call__(self, kernel, name, outs, scalars, arrays, scratch=(), alias=None, stored=(), inside=True, mib=8):
        count, waits = len(scalars) + len(arrays) + len(stored), len(self.last) + len(self.also)

        def body(*refs):
            kernel(*refs[:count], *refs[count + waits :])

        result = pl.pallas_call(
            body,
            in_specs=[SCALAR] * len(scalars) + [WHOLE] * len(arrays) + [ANYWHERE] * (len(stored) + waits),
            out_specs=[WHOLE] * len(outs),
            out_shape=[(pltpu.VMEM if inside else jax.ShapeDtypeStruct)(shape, dtype) for shape, dtype in outs],
            scratch_shapes=scratch,
            input_output_aliases=alias or {},
            compiler_params=pltpu.CompilerParams(vmem_limit_bytes=mib * 1024 * 1024),
            cost_estimate=pl.CostEstimate(flops=1, bytes_accessed=1, transcendentals=0),
            name=name,
        )(*scalars, *[near(a) for a in arrays], *[far_off(a) for a in stored], *self.last, *self.also)
        self.last, self.also = [result[0]], []
        return result


def own_kernel(sizes, me_ref, tokens_ref, ids_ref, weights_ref, own_ref, held, ids_held, weights_held, sems):
    width, row_count, experts = sizes
    extra = own_ref.shape[1] - width
    pairs = ((ids_ref, ids_held), (weights_ref, weights_held), (tokens_ref, held))
    copies = [pltpu.make_async_copy(source, target, sems.at[i]) for i, (source, target) in enumerate(pairs)]
    for copy in copies:
        copy.start()
    column = lax.broadcasted_iota(jnp.int32, (extra, row_count), 0)
    row = lax.broadcasted_iota(jnp.int32, (row_count, row_count), 0)
    other = lax.broadcasted_iota(jnp.int32, (row_count, row_count), 1)
    earlier = jnp.where(row < other, 1.0, 0.0).astype(BF16)
    same = jnp.where(row == other, 1.0, 0.0).astype(BF16)
    copies[0].wait()
    copies[1].wait()
    for s in range(held.shape[0]):
        present = jnp.zeros((extra, row_count), F32)
        weight = jnp.zeros((extra, row_count), F32)
        for k in range(ids_held.shape[1]):
            named = lax.rem(column, experts) == ids_held[s, k : k + 1, :]
            present = jnp.where(named, 1.0, present)
            weight = jnp.where(named, weights_held[s, k : k + 1, :], weight)
        before = jnp.dot(present.astype(BF16), earlier, preferred_element_type=F32)
        slot = jnp.where(present > 0.0, before, -1.0)
        high = weight.astype(BF16).astype(F32)
        value = jnp.where(column < experts, slot, jnp.where(column < 2 * experts, high, weight - high))
        turned = lax.dot_general(
            same, value.astype(BF16), (((1,), (1,)), ((), ())), preferred_element_type=F32
        )
        own_ref[s * row_count : (s + 1) * row_count, width:] = turned.astype(BF16)
    copies[2].wait()
    for s in range(held.shape[0]):
        own_ref[s * row_count : (s + 1) * row_count, :width] = held[s]


def loading(weights_ref, held_ref, sems):
    pieces = sems.shape[0]
    rows = weights_ref.shape[1] // pieces
    copies = []
    for i in range(pieces):
        part = (slice(None), pl.ds(i * rows, rows))
        copies.append(pltpu.make_async_copy(weights_ref.at[part], held_ref.at[part], sems.at[i]))
    return copies


def load_kernel(weights_ref, held_ref, sems):
    copies = loading(weights_ref, held_ref, sems)
    for copy in copies:
        copy.start()
    for copy in copies:
        copy.wait()


def pick(columns, lane_index):
    lane = lax.broadcasted_iota(jnp.int32, columns.shape, 1)
    return jnp.sum(jnp.where(lane == lane_index, columns, 0.0), axis=1, keepdims=True)


def placing(columns, expert, first_row, slots, row_count, capacity):
    rows = columns.shape[0]
    slot = pick(columns, expert).astype(jnp.int32)
    row = lax.broadcasted_iota(jnp.int32, (rows, 1), 0) + first_row
    target = jnp.where(slot >= 0, row // row_count * capacity + slot, -1)
    lane = lax.broadcasted_iota(jnp.int32, (rows, slots), 1)
    return jnp.where(lane == target, 1.0, 0.0).astype(BF16)


def gate_kernel(given_ref, out_ref):
    pass


def pack_kernel(*refs):
    *parts, out = refs
    start = 0
    for part in parts:
        rows = part.shape[0]
        out[start : start + rows, :] = part[...]
        start += rows


def dispatch_kernel(sizes, me_ref, *refs):
    (width, row_count, capacity, block), places = sizes
    *refs, own_ref, other_ref = refs
    parts = [(refs[i // 2], at) for i, at in enumerate(places)]
    slots = own_ref.shape[0]
    quarter = slots // 4
    for out, expert in ((own_ref, me_ref[0]), (other_ref, me_ref[0] ^ 1)):
        place = [
            placing(ref[at : at + block, width:].astype(F32), expert, 0, 128, row_count, capacity) for ref, at in parts
        ]
        place = jnp.concatenate(place, axis=0).T
        for i, (ref, at) in enumerate(parts):
            out[i * quarter : (i + 1) * quarter, :] = jnp.dot(
                place[:quarter, i * block : (i + 1) * block], ref[at : at + block, :], preferred_element_type=F32
            ).astype(BF16)


def expert_kernel(experts, me_ref, own_ref, got_ref, gate_ref, up_ref, down_ref, *refs):
    if len(refs) > 4:
        mine_ref, sent_ref, held_ref, rows_ref, hidden, sems = refs
        copies = loading(down_ref, held_ref, sems)
        down_ref = held_ref
    else:
        mine_ref, sent_ref, rows_ref, hidden = refs
        copies = []
    for copy in copies:
        copy.start()
    _, width, units = gate_ref.shape
    slots = own_ref.shape[0]
    rows_ref[:slots, :] = own_ref[...]
    rows_ref[slots:, :] = got_ref[...]
    columns = rows_ref[:, width:].astype(F32)
    weight = pick(columns, me_ref[0] + experts) + pick(columns, me_ref[0] + 2 * experts)
    tile = 256
    for j in range(0, units, tile):
        rows = rows_ref[:, :width]
        gate_val = jnp.dot(rows, gate_ref[0, :, j : j + tile], preferred_element_type=F32)
        up_val = jnp.dot(rows, up_ref[0, :, j : j + tile], preferred_element_type=F32)
        hidden[:, j : j + tile] = (gate_val / (1.0 + jnp.exp(-gate_val)) * up_val).astype(BF16)
    for copy in copies:
        copy.wait()
    tile = 512
    for n in range(0, width, tile):
        value = jnp.dot(hidden[...], down_ref[0, :, n : n + tile], preferred_element_type=F32)
        value = (value * weight).astype(BF16)
        mine_ref[:, n : n + tile] = value[:slots]
        sent_ref[:, n : n + tile] = value[slots:]


def shared_kernel(sizes, *refs):
    (width, _, _, block), places = sizes
    *refs, first_ref, second_ref, up_ref, out_ref, held_ref, rows_ref, sems = refs
    copies = loading(up_ref, held_ref, sems)
    for copy in copies:
        copy.start()
    for i, at in enumerate(places):
        ref = refs[i // 2]
        rows_ref[i * block : (i + 1) * block, :] = ref[at : at + block, :width]
    hidden = []
    for part in (first_ref, second_ref):
        gate_val = jnp.dot(rows_ref[...], part[0], preferred_element_type=F32)
        up_val = jnp.dot(rows_ref[...], part[1], preferred_element_type=F32)
        hidden.append((gate_val / (1.0 + jnp.exp(-gate_val)) * up_val).astype(BF16))
    tile = 512
    for n in range(0, width, tile):
        value = 0.0
        for h, part in zip(hidden, (first_ref, second_ref)):
            value += lax.dot_general(
                h, part[2, n : n + tile, :], (((1,), (1,)), ((), ())), preferred_element_type=F32
            )
        out_ref[:, n : n + tile] = value
    for copy in copies:
        copy.wait()


def combine_kernel(sizes, me_ref, *refs):
    (width, row_count, capacity, block), all_places, shared_at = sizes
    *refs, keep_ref, send_ref = refs
    count = len(all_places)
    tile = 512
    for c, places in enumerate(all_places):
        *parts, mine_ref, back_ref = refs[4 * c : 4 * c + 4]
        quarter = mine_ref.shape[0] // 4
        for i, at in enumerate(places):
            columns = parts[i // 2][at : at + block, width:].astype(F32)
            here = [placing(columns, e, 0, quarter, row_count, capacity) for e in (me_ref[0], me_ref[0] ^ 1)]
            out = (keep_ref, send_ref)[i // 2]
            first = (i % 2 * count + c) * block
            for n in range(0, width, tile):
                value = sum(
                    jnp.dot(p, part[i * quarter : (i + 1) * quarter, n : n + tile], preferred_element_type=F32)
                    for p, part in zip(here, (mine_ref, back_ref))
                )
                if c == shared_at:
                    value += refs[-1][i * block : (i + 1) * block, n : n + tile]
                out[first : first + block, n : n + tile] = value.astype(out.dtype)


def middle_kernel(keep_ref, got_ref, rest_ref, send_ref):
    half = rest_ref.shape[0]
    rest_ref[...] = keep_ref[:half, :] + got_ref[:half, :].astype(F32)
    send_ref[...] = (keep_ref[half:, :] + got_ref[half:, :].astype(F32)).astype(BF16)


def sum_kernel(pieces, *refs):
    *parts, out = refs
    rows = out.shape[0] // len(pieces) if out.ndim == 2 else out.shape[0] * out.shape[1]
    for i, piece in enumerate(pieces):
        total = sum(parts[p][at : at + rows, :].astype(F32) for p, at in piece).astype(BF16)
        if out.ndim == 2:
            out[i * rows : (i + 1) * rows, :] = total
        else:
            out[...] = total.reshape(out.shape)


def shards(tokens, expert_ids, combine_weights, w_gate, w_up, w_down, shared_weights):
    step_count, row_count, width = tokens.shape
    top_count = expert_ids.shape[2]
    devices = lax.axis_size(AXIS)
    experts = w_gate.shape[0] * devices
    capacity = max(2, row_count * top_count * 2 // experts)
    planes = devices // GROUP
    units = w_gate.shape[2]
    index = lax.axis_index(AXIS)[None].astype(jnp.int32)
    block = step_count * row_count
    rows = GROUP // 2 * block
    slots = rows // row_count * capacity
    full = width + (3 * experts + 127) // 128 * 128
    sizes = (width, row_count, capacity, block)
    line = Line()

    turned_shape = (step_count, top_count, row_count)
    own, = line(
        functools.partial(own_kernel, (width, row_count, experts)),
        "own",
        [((block, full), BF16)],
        [index],
        [],
        stored=[tokens, expert_ids.transpose(0, 2, 1), combine_weights.transpose(0, 2, 1)],
        scratch=[
            pltpu.VMEM(tokens.shape, BF16),
            pltpu.VMEM(turned_shape, jnp.int32),
            pltpu.VMEM(turned_shape, F32),
            pltpu.SemaphoreType.DMA((3,)),
        ],
    )
    shared_other = other_core(shared_weights)
    gather_groups, reduce_groups, order = (GATHER_GROUPS, REDUCE_GROUPS, ORDER) if planes == 4 else any_groups(planes)
    home = {k: (g, i, len(group)) for g, group in enumerate(gather_groups) for i, k in enumerate(group)}
    paired = any(1 in group and 3 in group for group in gather_groups)
    far = {0: own}
    for k in range(2, planes, 2):
        far[k] = across(own, k)
    if not paired:
        far[1] = across(own, 1)
    held = {}
    hop, wide, leaving, chosen, mine, back, got, rest, last, arrived, packed, kept = ({} for _ in range(12))

    def load(name, weights):
        held[name], = line(
            load_kernel,
            "load",
            [(weights.shape, BF16)],
            [],
            [],
            stored=[weights],
            scratch=[pltpu.SemaphoreType.DMA((4,))],
        )

    def enter(g):
        group = gather_groups[g]
        if paired and 1 in group:
            near_far, = line(pack_kernel, "pack", [((2 * block, full), BF16)], [], [own, far[2]])
            packed[g] = across(near_far, 1)
            packed[g], = line(gate_kernel, "enter", [(packed[g].shape, BF16)], [], [packed[g]], alias={0: 0})
        elif len(group) > 1:
            packed[g], = line(
                pack_kernel, "pack", [((len(group) * block, full), BF16)], [], [far[k] for k in group]
            )
        elif group[0] > 0:
            k = group[0]
            packed[g], = line(gate_kernel, "enter", [((block, full), BF16)], [], [far[k]], alias={0: 0})
            far[k] = packed[g]
        else:
            packed[g] = own
        for k in group:
            if not paired and k >= 2 and k & 1 == 0:
                far[k + 1] = across(far[k], 1)
        hop[g] = first_hop(packed[g])

    def pack(g):
        count = 2 * len(gather_groups[g])
        packed[g], = line(pack_kernel, "pack", [((count * block, full), BF16)], [], [packed[g], hop[g]])
        wide[g] = second_hop(packed[g])

    def blocks(k):
        g, i, n = home[k]
        places = (i * block, (n + i) * block)
        return [packed[g], wide[g]], places * 2

    def dispatch(k):
        arrays, places = blocks(k)
        chosen[k], out = line(
            functools.partial(dispatch_kernel, (sizes, places)),
            "dispatch",
            [((slots, full), BF16)] * 2,
            [index],
            arrays,
        )
        leaving[k] = other_core(out)

    def expert(k):
        loads_down = "down" not in held
        arrays = [chosen[k], leaving[k], held["gate"], held["up"]]
        mine[k], out, *brought = line(
            functools.partial(expert_kernel, experts),
            "expert_load" if loads_down else "expert",
            [((slots, width), BF16)] * 2 + [(w_down.shape, BF16)] * loads_down,
            [index],
            arrays if loads_down else arrays + [held["down"]],
            stored=[w_down] if loads_down else [],
            scratch=[pltpu.VMEM((2 * slots, full), BF16), pltpu.VMEM((2 * slots, units), BF16)]
            + [pltpu.SemaphoreType.DMA((4,))] * loads_down,
        )
        if loads_down:
            held["down"], = brought
        back[k] = other_core(out)

    def shared():
        arrays, places = blocks(0)
        kept["shared"], held["up"] = line(
            functools.partial(shared_kernel, (sizes, places)),
            "shared",
            [((rows, width), F32), (w_up.shape, BF16)],
            [],
            [*arrays, shared_weights, shared_other],
            stored=[w_up],
            scratch=[pltpu.VMEM((rows, width), BF16), pltpu.SemaphoreType.DMA((4,))],
        )

    def combine(r):
        group = reduce_groups[r]
        arrays, all_places = [], []
        for k in group:
            pair, places = blocks(k)
            arrays += [*pair, mine[k], back[k]]
            all_places.append(places)
        shared_at = group.index(0) if 0 in group else -1
        if 0 in group:
            arrays.append(kept["shared"])
        half = 2 * block * len(group)
        kept[r], send = line(
            functools.partial(combine_kernel, (sizes, all_places, shared_at)),
            f"combine{len(group)}",
            [((half, width), F32), ((half, width), BF16)],
            [index],
            arrays,
        )
        got[r] = second_hop(send)

    def middle(r):
        half = block * len(reduce_groups[r])
        rest[r], send = line(
            middle_kernel, "middle", [((half, width), F32), ((half, width), BF16)], [], [kept[r], got[r]]
        )
        last[r] = first_hop(send)

    def leave(r):
        group = reduce_groups[r]
        for k in group:
            if k == 0 or (k == 3 and 1 in group):
                continue
            both = [k, 3] if k == 1 and 3 in group else [k]
            arrays, pieces = [rest[r], last[r]], []
            for j in both:
                at = group.index(j) * block
                pieces.append([(0, at), (1, at)])
            if k >= 2 and k & 1 == 0:
                array, at = arrived.pop(k + 1)
                arrays.append(array)
                pieces[0].append((2, at))
            out, = line(
                functools.partial(sum_kernel, pieces), "leave", [((len(both) * block, width), BF16)], [], arrays
            )
            out = across(out, 1 if k & 1 else k)
            for i, j in enumerate(both):
                arrived[j] = (out, i * block)

    def final():
        r = [r for r, group in enumerate(reduce_groups) if 0 in group][0]
        at = reduce_groups[r].index(0) * block
        arrays, pieces = [rest[r], last[r]], [(0, at), (1, at)]
        for array, at in arrived.values():
            pieces.append((len(arrays), at))
            arrays.append(array)
        out, = line(
            functools.partial(sum_kernel, [pieces]),
            "final",
            [((step_count, row_count, width), BF16)],
            [],
            arrays,
            inside=False,
        )
        return out

    steps = {
        "E": enter,
        "K": pack,
        "L": lambda i: load("gate", w_gate),
        "D": dispatch,
        "X": expert,
        "S": lambda i: shared(),
        "C": combine,
        "M": middle,
        "V": leave,
    }
    stores = {"h": hop, "w": wide, "c": leaving, "b": back, "g": got, "l": last}
    for step in order:
        step, *also = step.split(":")
        line.also = [stores[name[0]][int(name[1:])] for name in also]
        steps[step[0]](int(step[1:]))
    return final()


def solution(mesh):
    placed = (
        P(None, AXIS, None),
        P(None, AXIS, None),
        P(None, AXIS, None),
        P(AXIS, None, None),
        P(AXIS, None, None),
        P(AXIS, None, None),
        P(None, None, AXIS),
    )
    return jax.shard_map(
        shards, mesh=mesh, in_specs=placed, out_specs=P(None, AXIS, None), check_vma=False
    )
```

```python
import functools

import jax
import jax.numpy as jnp
from jax import lax
from jax.experimental import pallas as pl
from jax.experimental.pallas import tpu as pltpu
from jax.sharding import PartitionSpec as P

AXIS = "ep"
GROUP = 8
WHOLE = pl.BlockSpec(memory_space=pltpu.VMEM)
ANYWHERE = pl.BlockSpec(memory_space=pl.ANY)
SCALAR = pl.BlockSpec(memory_space=pltpu.SMEM)
F32, BF16 = jnp.float32, jnp.bfloat16


def swap(block, mask_even, mask_odd):
    count = lax.axis_size(AXIS)
    route = [(i, i ^ (mask_odd if i & 1 else mask_even)) for i in range(count)]
    return lax.ppermute(block, AXIS, route)


def first_hop(block):
    return swap(block, 2, 4)


def second_hop(block):
    return swap(block, 4, 2)


def across(block, k):
    return swap(block, GROUP * k, GROUP * k)


def other_core(block):
    return swap(block, 1, 1)


def far_off(array):
    return pltpu.with_memory_space_constraint(array, pltpu.HBM)


def near(array):
    return pltpu.with_memory_space_constraint(array, pltpu.VMEM)


ORDER = (
    "E0", "K0", "L0", "E1", "E2", "K1", "K2", "S0", "E3", "D0:h1", "L1:w0", "D1", "K3", "D2", "X1",
    "X2", "D3", "C0:w2", "X3", "C1", "X0", "M0", "C2", "M1", "V0", "C3:h1", "M2", "V2", "M3",
)
GATHER_GROUPS = ((0,), (1,), (2,), (3,))
DIRECT = True
REDUCE_GROUPS = ((2,), (1,), (3,), (0,))


def any_groups(planes):
    gather = tuple((k,) for k in range(planes))
    reduce = tuple((k,) for k in reversed(range(planes)))
    steps = ["E0", "K0", "L0", "L1"]
    for k in range(1, planes):
        steps += [f"E{k}", f"K{k}"]
    steps += ["S0"]
    for i, (k,) in enumerate(reduce):
        steps += [f"D{k}", f"X{k}", f"C{i}", f"M{i}", f"V{i}"]
    return gather, reduce, steps


class Line:
    def __init__(self):
        self.last = []
        self.also = []

    def __call__(self, kernel, name, outs, scalars, arrays, scratch=(), alias=None, stored=(), inside=True, mib=8):
        count, waits = len(scalars) + len(arrays) + len(stored), len(self.last) + len(self.also)

        def body(*refs):
            kernel(*refs[:count], *refs[count + waits :])

        result = pl.pallas_call(
            body,
            in_specs=[SCALAR] * len(scalars) + [WHOLE] * len(arrays) + [ANYWHERE] * (len(stored) + waits),
            out_specs=[WHOLE] * len(outs),
            out_shape=[(pltpu.VMEM if inside else jax.ShapeDtypeStruct)(shape, dtype) for shape, dtype in outs],
            scratch_shapes=scratch,
            input_output_aliases=alias or {},
            compiler_params=pltpu.CompilerParams(vmem_limit_bytes=mib * 1024 * 1024),
            cost_estimate=pl.CostEstimate(flops=1, bytes_accessed=1, transcendentals=0),
            name=name,
        )(*scalars, *[near(a) for a in arrays], *[far_off(a) for a in stored], *self.last, *self.also)
        self.last, self.also = [result[0]], []
        return result


def own_kernel(sizes, me_ref, tokens_ref, ids_ref, weights_ref, own_ref, held, ids_held, weights_held, sems):
    width, row_count, experts = sizes
    extra = own_ref.shape[1] - width
    pairs = ((ids_ref, ids_held), (weights_ref, weights_held), (tokens_ref, held))
    copies = [pltpu.make_async_copy(source, target, sems.at[i]) for i, (source, target) in enumerate(pairs)]
    for copy in copies:
        copy.start()
    column = lax.broadcasted_iota(jnp.int32, (extra, row_count), 0)
    row = lax.broadcasted_iota(jnp.int32, (row_count, row_count), 0)
    other = lax.broadcasted_iota(jnp.int32, (row_count, row_count), 1)
    earlier = jnp.where(row < other, 1.0, 0.0).astype(BF16)
    same = jnp.where(row == other, 1.0, 0.0).astype(BF16)
    copies[0].wait()
    copies[1].wait()
    for s in range(held.shape[0]):
        present = jnp.zeros((extra, row_count), F32)
        weight = jnp.zeros((extra, row_count), F32)
        for k in range(ids_held.shape[1]):
            named = lax.rem(column, experts) == ids_held[s, k : k + 1, :]
            present = jnp.where(named, 1.0, present)
            weight = jnp.where(named, weights_held[s, k : k + 1, :], weight)
        before = jnp.dot(present.astype(BF16), earlier, preferred_element_type=F32)
        slot = jnp.where(present > 0.0, before, -1.0)
        high = weight.astype(BF16).astype(F32)
        value = jnp.where(column < experts, slot, jnp.where(column < 2 * experts, high, weight - high))
        turned = lax.dot_general(
            same, value.astype(BF16), (((1,), (1,)), ((), ())), preferred_element_type=F32
        )
        own_ref[s * row_count : (s + 1) * row_count, width:] = turned.astype(BF16)
    copies[2].wait()
    for s in range(held.shape[0]):
        own_ref[s * row_count : (s + 1) * row_count, :width] = held[s]


def loading(weights_ref, held_ref, sems):
    pieces = sems.shape[0]
    rows = weights_ref.shape[1] // pieces
    copies = []
    for i in range(pieces):
        part = (slice(None), pl.ds(i * rows, rows))
        copies.append(pltpu.make_async_copy(weights_ref.at[part], held_ref.at[part], sems.at[i]))
    return copies


def load_kernel(weights_ref, held_ref, sems):
    copies = loading(weights_ref, held_ref, sems)
    for copy in copies:
        copy.start()
    for copy in copies:
        copy.wait()


def pick(columns, lane_index):
    lane = lax.broadcasted_iota(jnp.int32, columns.shape, 1)
    return jnp.sum(jnp.where(lane == lane_index, columns, 0.0), axis=1, keepdims=True)


def placing(columns, expert, first_row, slots, row_count, capacity):
    rows = columns.shape[0]
    slot = pick(columns, expert).astype(jnp.int32)
    row = lax.broadcasted_iota(jnp.int32, (rows, 1), 0) + first_row
    target = jnp.where(slot >= 0, row // row_count * capacity + slot, -1)
    lane = lax.broadcasted_iota(jnp.int32, (rows, slots), 1)
    return jnp.where(lane == target, 1.0, 0.0).astype(BF16)


def gate_kernel(given_ref, out_ref):
    pass


def pack_kernel(*refs):
    *parts, out = refs
    start = 0
    for part in parts:
        rows = part.shape[0]
        out[start : start + rows, :] = part[...]
        start += rows


def dispatch_kernel(sizes, me_ref, *refs):
    (width, row_count, capacity, block), places = sizes
    *refs, own_ref, other_ref = refs
    parts = [(refs[i // 2], at) for i, at in enumerate(places)]
    slots = own_ref.shape[0]
    quarter = slots // 4
    for out, expert in ((own_ref, me_ref[0]), (other_ref, me_ref[0] ^ 1)):
        place = [
            placing(ref[at : at + block, width:].astype(F32), expert, 0, 128, row_count, capacity) for ref, at in parts
        ]
        place = jnp.concatenate(place, axis=0).T
        for i, (ref, at) in enumerate(parts):
            out[i * quarter : (i + 1) * quarter, :] = jnp.dot(
                place[:quarter, i * block : (i + 1) * block], ref[at : at + block, :], preferred_element_type=F32
            ).astype(BF16)


def expert_kernel(experts, me_ref, own_ref, got_ref, gate_ref, up_ref, down_ref, mine_ref, sent_ref, rows_ref, hidden):
    _, width, units = gate_ref.shape
    slots = own_ref.shape[0]
    rows_ref[:slots, :] = own_ref[...]
    rows_ref[slots:, :] = got_ref[...]
    columns = rows_ref[:, width:].astype(F32)
    weight = pick(columns, me_ref[0] + experts) + pick(columns, me_ref[0] + 2 * experts)
    tile = 256
    for j in range(0, units, tile):
        rows = rows_ref[:, :width]
        gate_val = jnp.dot(rows, gate_ref[0, :, j : j + tile], preferred_element_type=F32)
        up_val = jnp.dot(rows, up_ref[0, :, j : j + tile], preferred_element_type=F32)
        hidden[:, j : j + tile] = (gate_val / (1.0 + jnp.exp(-gate_val)) * up_val).astype(BF16)
    tile = 512
    for n in range(0, width, tile):
        value = jnp.dot(hidden[...], down_ref[0, :, n : n + tile], preferred_element_type=F32)
        value = (value * weight).astype(BF16)
        mine_ref[:, n : n + tile] = value[:slots]
        sent_ref[:, n : n + tile] = value[slots:]


def shared_kernel(sizes, *refs):
    (width, _, _, block), places = sizes
    *refs, first_ref, second_ref, up_ref, out_ref, held_ref, rows_ref, sems = refs
    copies = loading(up_ref, held_ref, sems)
    for copy in copies:
        copy.start()
    for i, at in enumerate(places):
        ref = refs[i // 2]
        rows_ref[i * block : (i + 1) * block, :] = ref[at : at + block, :width]
    hidden = []
    for part in (first_ref, second_ref):
        gate_val = jnp.dot(rows_ref[...], part[0], preferred_element_type=F32)
        up_val = jnp.dot(rows_ref[...], part[1], preferred_element_type=F32)
        hidden.append((gate_val / (1.0 + jnp.exp(-gate_val)) * up_val).astype(BF16))
    tile = 512
    for n in range(0, width, tile):
        value = 0.0
        for h, part in zip(hidden, (first_ref, second_ref)):
            value += lax.dot_general(
                h, part[2, n : n + tile, :], (((1,), (1,)), ((), ())), preferred_element_type=F32
            )
        out_ref[:, n : n + tile] = value
    for copy in copies:
        copy.wait()


def combine_kernel(sizes, me_ref, *refs):
    (width, row_count, capacity, block), all_places, shared_at = sizes
    *refs, keep_ref, send_ref = refs
    count = len(all_places)
    tile = 512
    for c, places in enumerate(all_places):
        *parts, mine_ref, back_ref = refs[4 * c : 4 * c + 4]
        quarter = mine_ref.shape[0] // 4
        for i, at in enumerate(places):
            columns = parts[i // 2][at : at + block, width:].astype(F32)
            here = [placing(columns, e, 0, quarter, row_count, capacity) for e in (me_ref[0], me_ref[0] ^ 1)]
            out = (keep_ref, send_ref)[i // 2]
            first = (i % 2 * count + c) * block
            for n in range(0, width, tile):
                value = sum(
                    jnp.dot(p, part[i * quarter : (i + 1) * quarter, n : n + tile], preferred_element_type=F32)
                    for p, part in zip(here, (mine_ref, back_ref))
                )
                if c == shared_at:
                    value += refs[-1][i * block : (i + 1) * block, n : n + tile]
                out[first : first + block, n : n + tile] = value.astype(out.dtype)


def middle_kernel(keep_ref, got_ref, *refs):
    *more, rest_ref, send_ref = refs
    half = rest_ref.shape[0]
    parts = [got_ref, *more]
    rest_ref[...] = keep_ref[:half, :] + sum(part[:half, :].astype(F32) for part in parts)
    send_ref[...] = (keep_ref[half:, :] + sum(part[half:, :].astype(F32) for part in parts)).astype(BF16)


def sum_kernel(pieces, *refs):
    *parts, out = refs
    rows = out.shape[0] // len(pieces) if out.ndim == 2 else out.shape[0] * out.shape[1]
    for i, piece in enumerate(pieces):
        total = sum(parts[p][at : at + rows, :].astype(F32) for p, at in piece).astype(BF16)
        if out.ndim == 2:
            out[i * rows : (i + 1) * rows, :] = total
        else:
            out[...] = total.reshape(out.shape)


def shards(tokens, expert_ids, combine_weights, w_gate, w_up, w_down, shared_weights):
    step_count, row_count, width = tokens.shape
    top_count = expert_ids.shape[2]
    devices = lax.axis_size(AXIS)
    experts = w_gate.shape[0] * devices
    capacity = max(2, row_count * top_count * 2 // experts)
    planes = devices // GROUP
    units = w_gate.shape[2]
    index = lax.axis_index(AXIS)[None].astype(jnp.int32)
    block = step_count * row_count
    rows = GROUP // 2 * block
    slots = rows // row_count * capacity
    full = width + (3 * experts + 127) // 128 * 128
    sizes = (width, row_count, capacity, block)
    line = Line()

    turned_shape = (step_count, top_count, row_count)
    own, = line(
        functools.partial(own_kernel, (width, row_count, experts)),
        "own",
        [((block, full), BF16)],
        [index],
        [],
        stored=[tokens, expert_ids.transpose(0, 2, 1), combine_weights.transpose(0, 2, 1)],
        scratch=[
            pltpu.VMEM(tokens.shape, BF16),
            pltpu.VMEM(turned_shape, jnp.int32),
            pltpu.VMEM(turned_shape, F32),
            pltpu.SemaphoreType.DMA((3,)),
        ],
    )
    shared_other = other_core(shared_weights)
    gather_groups, reduce_groups, order = (GATHER_GROUPS, REDUCE_GROUPS, ORDER) if planes == 4 else any_groups(planes)
    home = {k: (g, i, len(group)) for g, group in enumerate(gather_groups) for i, k in enumerate(group)}
    paired = any(1 in group and 3 in group for group in gather_groups)
    far = {0: own}
    for k in range(2, planes, 2):
        far[k] = across(own, k)
    if not paired:
        far[1] = across(own, 1)
    held = {}
    hop, wide, leaving, chosen, mine, back, got, rest, last, arrived, packed, kept, coming, crossed = ({} for _ in range(14))

    def load(name, weights):
        held[name], = line(
            load_kernel,
            "load",
            [(weights.shape, BF16)],
            [],
            [],
            stored=[weights],
            scratch=[pltpu.SemaphoreType.DMA((4,))],
        )

    def enter(g):
        group = gather_groups[g]
        if paired and 1 in group:
            near_far, = line(pack_kernel, "pack", [((2 * block, full), BF16)], [], [own, far[2]])
            packed[g] = across(near_far, 1)
            packed[g], = line(gate_kernel, "enter", [(packed[g].shape, BF16)], [], [packed[g]], alias={0: 0})
        elif len(group) > 1:
            packed[g], = line(
                pack_kernel, "pack", [((len(group) * block, full), BF16)], [], [far[k] for k in group]
            )
        elif group[0] > 0:
            k = group[0]
            packed[g], = line(gate_kernel, "enter", [((block, full), BF16)], [], [far[k]], alias={0: 0})
            far[k] = packed[g]
        else:
            packed[g] = own
        for k in group:
            if not paired and k >= 2 and k & 1 == 0:
                far[k + 1] = across(far[k], 1)
        hop[g] = first_hop(packed[g])

    def pack(g):
        count = 2 * len(gather_groups[g])
        packed[g], = line(pack_kernel, "pack", [((count * block, full), BF16)], [], [packed[g], hop[g]])
        wide[g] = second_hop(packed[g])

    def blocks(k):
        g, i, n = home[k]
        places = (i * block, (n + i) * block)
        return [packed[g], wide[g]], places * 2

    def dispatch(k):
        arrays, places = blocks(k)
        chosen[k], out = line(
            functools.partial(dispatch_kernel, (sizes, places)),
            "dispatch",
            [((slots, full), BF16)] * 2,
            [index],
            arrays,
        )
        leaving[k] = other_core(out)

    def expert(k):
        mine[k], out = line(
            functools.partial(expert_kernel, experts),
            "expert",
            [((slots, width), BF16)] * 2,
            [index],
            [chosen[k], leaving[k], held["gate"], held["up"], held["down"]],
            scratch=[pltpu.VMEM((2 * slots, full), BF16), pltpu.VMEM((2 * slots, units), BF16)],
        )
        back[k] = other_core(out)

    def shared():
        arrays, places = blocks(0)
        kept["shared"], held["up"] = line(
            functools.partial(shared_kernel, (sizes, places)),
            "shared",
            [((rows, width), F32), (w_up.shape, BF16)],
            [],
            [*arrays, shared_weights, shared_other],
            stored=[w_up],
            scratch=[pltpu.VMEM((rows, width), BF16), pltpu.SemaphoreType.DMA((4,))],
        )

    def combine(r):
        group = reduce_groups[r]
        arrays, all_places = [], []
        for k in group:
            pair, places = blocks(k)
            arrays += [*pair, mine[k], back[k]]
            all_places.append(places)
        shared_at = group.index(0) if 0 in group else -1
        if 0 in group:
            arrays.append(kept["shared"])
        half = 2 * block * len(group)
        kept[r], send = line(
            functools.partial(combine_kernel, (sizes, all_places, shared_at)),
            f"combine{len(group)}",
            [((half, width), F32), ((half, width), BF16)],
            [index],
            arrays,
        )
        got[r] = second_hop(send)

    def middle(r):
        group = reduce_groups[r]
        if group == (1,):
            out, = line(
                functools.partial(sum_kernel, [[(0, 0), (1, 0)]]),
                "sum",
                [((2 * block, width), BF16)],
                [],
                [kept[r], got[r]],
            )
            crossed[1] = across(out, 1)
            return
        half = block * len(group)
        rest[r], send = line(
            middle_kernel,
            "middle",
            [((half, width), F32), ((half, width), BF16)],
            [],
            [kept[r], got[r]] + ([crossed[1]] if 0 in group else []),
        )
        last[r] = first_hop(send)

    def leave(r):
        group = reduce_groups[r]
        for k in group:
            if k < 2:
                continue
            both = [k]
            arrays, pieces = [rest[r], last[r]], []
            for j in both:
                at = group.index(j) * block
                pieces.append([(0, at), (1, at)])
            if k >= 2 and k & 1 == 0 and not DIRECT:
                array, at = arrived.pop(k + 1)
                arrays.append(array)
                pieces[0].append((2, at))
            out, = line(
                functools.partial(sum_kernel, pieces), "leave", [((len(both) * block, width), BF16)], [], arrays
            )
            out = across(out, 1 if k & 1 and not DIRECT else k)
            for i, j in enumerate(both):
                arrived[j] = (out, i * block)
                coming[j] = out

    def final():
        r = [r for r, group in enumerate(reduce_groups) if 0 in group][0]
        at = reduce_groups[r].index(0) * block
        arrays, pieces = [rest[r], last[r]], [(0, at), (1, at)]
        for array, at in arrived.values():
            pieces.append((len(arrays), at))
            arrays.append(array)
        out, = line(
            functools.partial(sum_kernel, [pieces]),
            "final",
            [((step_count, row_count, width), BF16)],
            [],
            arrays,
            inside=False,
        )
        return out

    steps = {
        "E": enter,
        "K": pack,
        "L": lambda i: load("down", w_down) if i else load("gate", w_gate),
        "D": dispatch,
        "X": expert,
        "S": lambda i: shared(),
        "C": combine,
        "M": middle,
        "V": leave,
    }
    stores = {"h": hop, "w": wide, "c": leaving, "b": back, "g": got, "l": last, "a": coming, "z": crossed}
    for step in order:
        step, *also = step.split(":")
        line.also = [stores[name[0]][int(name[1:])] for name in also]
        steps[step[0]](int(step[1:]))
    return final()


def solution(mesh):
    placed = (
        P(None, AXIS, None),
        P(None, AXIS, None),
        P(None, AXIS, None),
        P(AXIS, None, None),
        P(AXIS, None, None),
        P(AXIS, None, None),
        P(None, None, AXIS),
    )
    return jax.shard_map(
        shards, mesh=mesh, in_specs=placed, out_specs=P(None, AXIS, None), check_vma=False
    )
```

```python
import functools

import jax
import jax.numpy as jnp
from jax import lax
from jax.experimental import pallas as pl
from jax.experimental.pallas import tpu as pltpu
from jax.sharding import PartitionSpec as P

AXIS = "ep"
GROUP = 8
WHOLE = pl.BlockSpec(memory_space=pltpu.VMEM)
ANYWHERE = pl.BlockSpec(memory_space=pl.ANY)
SCALAR = pl.BlockSpec(memory_space=pltpu.SMEM)
F32, BF16 = jnp.float32, jnp.bfloat16


def swap(block, mask_even, mask_odd):
    count = lax.axis_size(AXIS)
    route = [(i, i ^ (mask_odd if i & 1 else mask_even)) for i in range(count)]
    return lax.ppermute(block, AXIS, route)


def first_hop(block):
    return swap(block, 2, 4)


def second_hop(block):
    return swap(block, 4, 2)


def across(block, k):
    return swap(block, GROUP * k, GROUP * k)


def other_core(block):
    return swap(block, 1, 1)


def far_off(array):
    return pltpu.with_memory_space_constraint(array, pltpu.HBM)


def near(array):
    return pltpu.with_memory_space_constraint(array, pltpu.VMEM)


ORDER = (
    "E0", "K0", "L0", "E1", "E2", "K1", "K2", "S0", "E3", "D0:h1", "L1:w0", "D1", "K3", "D2", "X1",
    "X2", "D3", "C0:w2", "C1", "X3", "X0", "M0", "C2", "M1", "V0", "C3:h1", "M2", "V2", "M3",
)
GATHER_GROUPS = ((0,), (1,), (2,), (3,))
DIRECT = True
REDUCE_GROUPS = ((2,), (1,), (3,), (0,))


def any_groups(planes):
    gather = tuple((k,) for k in range(planes))
    reduce = tuple((k,) for k in reversed(range(planes)))
    steps = ["E0", "K0", "L0", "L1"]
    for k in range(1, planes):
        steps += [f"E{k}", f"K{k}"]
    steps += ["S0"]
    for i, (k,) in enumerate(reduce):
        steps += [f"D{k}", f"X{k}", f"C{i}", f"M{i}", f"V{i}"]
    return gather, reduce, steps


class Line:
    def __init__(self):
        self.last = []
        self.also = []

    def __call__(self, kernel, name, outs, scalars, arrays, scratch=(), alias=None, stored=(), inside=True, mib=8):
        count, waits = len(scalars) + len(arrays) + len(stored), len(self.last) + len(self.also)

        def body(*refs):
            kernel(*refs[:count], *refs[count + waits :])

        result = pl.pallas_call(
            body,
            in_specs=[SCALAR] * len(scalars) + [WHOLE] * len(arrays) + [ANYWHERE] * (len(stored) + waits),
            out_specs=[WHOLE] * len(outs),
            out_shape=[(pltpu.VMEM if inside else jax.ShapeDtypeStruct)(shape, dtype) for shape, dtype in outs],
            scratch_shapes=scratch,
            input_output_aliases=alias or {},
            compiler_params=pltpu.CompilerParams(vmem_limit_bytes=mib * 1024 * 1024),
            cost_estimate=pl.CostEstimate(flops=1, bytes_accessed=1, transcendentals=0),
            name=name,
        )(*scalars, *[near(a) for a in arrays], *[far_off(a) for a in stored], *self.last, *self.also)
        self.last, self.also = [result[0]], []
        return result


def own_kernel(sizes, me_ref, tokens_ref, ids_ref, weights_ref, own_ref, held, ids_held, weights_held, sems):
    width, row_count, experts = sizes
    extra = own_ref.shape[1] - width
    pairs = ((ids_ref, ids_held), (weights_ref, weights_held), (tokens_ref, held))
    copies = [pltpu.make_async_copy(source, target, sems.at[i]) for i, (source, target) in enumerate(pairs)]
    for copy in copies:
        copy.start()
    column = lax.broadcasted_iota(jnp.int32, (extra, row_count), 0)
    row = lax.broadcasted_iota(jnp.int32, (row_count, row_count), 0)
    other = lax.broadcasted_iota(jnp.int32, (row_count, row_count), 1)
    earlier = jnp.where(row < other, 1.0, 0.0).astype(BF16)
    same = jnp.where(row == other, 1.0, 0.0).astype(BF16)
    copies[0].wait()
    copies[1].wait()
    for s in range(held.shape[0]):
        present = jnp.zeros((extra, row_count), F32)
        weight = jnp.zeros((extra, row_count), F32)
        for k in range(ids_held.shape[1]):
            named = lax.rem(column, experts) == ids_held[s, k : k + 1, :]
            present = jnp.where(named, 1.0, present)
            weight = jnp.where(named, weights_held[s, k : k + 1, :], weight)
        before = jnp.dot(present.astype(BF16), earlier, preferred_element_type=F32)
        slot = jnp.where(present > 0.0, before, -1.0)
        high = weight.astype(BF16).astype(F32)
        value = jnp.where(column < experts, slot, jnp.where(column < 2 * experts, high, weight - high))
        turned = lax.dot_general(
            same, value.astype(BF16), (((1,), (1,)), ((), ())), preferred_element_type=F32
        )
        own_ref[s * row_count : (s + 1) * row_count, width:] = turned.astype(BF16)
    copies[2].wait()
    for s in range(held.shape[0]):
        own_ref[s * row_count : (s + 1) * row_count, :width] = held[s]


def loading(weights_ref, held_ref, sems):
    pieces = sems.shape[0]
    rows = weights_ref.shape[1] // pieces
    copies = []
    for i in range(pieces):
        part = (slice(None), pl.ds(i * rows, rows))
        copies.append(pltpu.make_async_copy(weights_ref.at[part], held_ref.at[part], sems.at[i]))
    return copies


def load_kernel(weights_ref, held_ref, sems):
    copies = loading(weights_ref, held_ref, sems)
    for copy in copies:
        copy.start()
    for copy in copies:
        copy.wait()


def pick(columns, lane_index):
    lane = lax.broadcasted_iota(jnp.int32, columns.shape, 1)
    return jnp.sum(jnp.where(lane == lane_index, columns, 0.0), axis=1, keepdims=True)


def placing(columns, expert, first_row, slots, row_count, capacity):
    rows = columns.shape[0]
    slot = pick(columns, expert).astype(jnp.int32)
    row = lax.broadcasted_iota(jnp.int32, (rows, 1), 0) + first_row
    target = jnp.where(slot >= 0, row // row_count * capacity + slot, -1)
    lane = lax.broadcasted_iota(jnp.int32, (rows, slots), 1)
    return jnp.where(lane == target, 1.0, 0.0).astype(BF16)


def gate_kernel(given_ref, out_ref):
    pass


def pack_kernel(*refs):
    *parts, out = refs
    start = 0
    for part in parts:
        rows = part.shape[0]
        out[start : start + rows, :] = part[...]
        start += rows


def dispatch_kernel(sizes, me_ref, *refs):
    (width, row_count, capacity, block), places = sizes
    *refs, own_ref, other_ref = refs
    parts = [(refs[i // 2], at) for i, at in enumerate(places)]
    slots = own_ref.shape[0]
    quarter = slots // 4
    for out, expert in ((own_ref, me_ref[0]), (other_ref, me_ref[0] ^ 1)):
        place = [
            placing(ref[at : at + block, width:].astype(F32), expert, 0, 128, row_count, capacity) for ref, at in parts
        ]
        place = jnp.concatenate(place, axis=0).T
        for i, (ref, at) in enumerate(parts):
            out[i * quarter : (i + 1) * quarter, :] = jnp.dot(
                place[:quarter, i * block : (i + 1) * block], ref[at : at + block, :], preferred_element_type=F32
            ).astype(BF16)


def expert_kernel(experts, me_ref, own_ref, got_ref, gate_ref, up_ref, down_ref, mine_ref, sent_ref, rows_ref, hidden):
    _, width, units = gate_ref.shape
    slots = own_ref.shape[0]
    rows_ref[:slots, :] = own_ref[...]
    rows_ref[slots:, :] = got_ref[...]
    columns = rows_ref[:, width:].astype(F32)
    weight = pick(columns, me_ref[0] + experts) + pick(columns, me_ref[0] + 2 * experts)
    tile = 256
    for j in range(0, units, tile):
        rows = rows_ref[:, :width]
        gate_val = jnp.dot(rows, gate_ref[0, :, j : j + tile], preferred_element_type=F32)
        up_val = jnp.dot(rows, up_ref[0, :, j : j + tile], preferred_element_type=F32)
        hidden[:, j : j + tile] = (gate_val / (1.0 + jnp.exp(-gate_val)) * up_val).astype(BF16)
    tile = 512
    for n in range(0, width, tile):
        value = jnp.dot(hidden[...], down_ref[0, :, n : n + tile], preferred_element_type=F32)
        value = (value * weight).astype(BF16)
        mine_ref[:, n : n + tile] = value[:slots]
        sent_ref[:, n : n + tile] = value[slots:]


def shared_kernel(sizes, *refs):
    (width, _, _, block), places = sizes
    *refs, first_ref, second_ref, up_ref, out_ref, held_ref, rows_ref, sems = refs
    copies = loading(up_ref, held_ref, sems)
    for copy in copies:
        copy.start()
    for i, at in enumerate(places):
        ref = refs[i // 2]
        rows_ref[i * block : (i + 1) * block, :] = ref[at : at + block, :width]
    hidden = []
    for part in (first_ref, second_ref):
        gate_val = jnp.dot(rows_ref[...], part[0], preferred_element_type=F32)
        up_val = jnp.dot(rows_ref[...], part[1], preferred_element_type=F32)
        hidden.append((gate_val / (1.0 + jnp.exp(-gate_val)) * up_val).astype(BF16))
    tile = 512
    for n in range(0, width, tile):
        value = 0.0
        for h, part in zip(hidden, (first_ref, second_ref)):
            value += lax.dot_general(
                h, part[2, n : n + tile, :], (((1,), (1,)), ((), ())), preferred_element_type=F32
            )
        out_ref[:, n : n + tile] = value
    for copy in copies:
        copy.wait()


def combine_kernel(sizes, me_ref, *refs):
    (width, row_count, capacity, block), all_places, shared_at = sizes
    *refs, keep_ref, send_ref = refs
    count = len(all_places)
    tile = 512
    for c, places in enumerate(all_places):
        *parts, mine_ref, back_ref = refs[4 * c : 4 * c + 4]
        quarter = mine_ref.shape[0] // 4
        for i, at in enumerate(places):
            columns = parts[i // 2][at : at + block, width:].astype(F32)
            here = [placing(columns, e, 0, quarter, row_count, capacity) for e in (me_ref[0], me_ref[0] ^ 1)]
            out = (keep_ref, send_ref)[i // 2]
            first = (i % 2 * count + c) * block
            for n in range(0, width, tile):
                value = sum(
                    jnp.dot(p, part[i * quarter : (i + 1) * quarter, n : n + tile], preferred_element_type=F32)
                    for p, part in zip(here, (mine_ref, back_ref))
                )
                if c == shared_at:
                    value += refs[-1][i * block : (i + 1) * block, n : n + tile]
                out[first : first + block, n : n + tile] = value.astype(out.dtype)


def middle_kernel(keep_ref, got_ref, *refs):
    *more, rest_ref, send_ref = refs
    half = rest_ref.shape[0]
    parts = [got_ref, *more]
    rest_ref[...] = keep_ref[:half, :] + sum(part[:half, :].astype(F32) for part in parts)
    send_ref[...] = (keep_ref[half:, :] + sum(part[half:, :].astype(F32) for part in parts)).astype(BF16)


def sum_kernel(pieces, *refs):
    *parts, out = refs
    rows = out.shape[0] // len(pieces) if out.ndim == 2 else out.shape[0] * out.shape[1]
    for i, piece in enumerate(pieces):
        total = sum(parts[p][at : at + rows, :].astype(F32) for p, at in piece).astype(BF16)
        if out.ndim == 2:
            out[i * rows : (i + 1) * rows, :] = total
        else:
            out[...] = total.reshape(out.shape)


def shards(tokens, expert_ids, combine_weights, w_gate, w_up, w_down, shared_weights):
    step_count, row_count, width = tokens.shape
    top_count = expert_ids.shape[2]
    devices = lax.axis_size(AXIS)
    experts = w_gate.shape[0] * devices
    capacity = max(2, row_count * top_count * 2 // experts)
    planes = devices // GROUP
    units = w_gate.shape[2]
    index = lax.axis_index(AXIS)[None].astype(jnp.int32)
    block = step_count * row_count
    rows = GROUP // 2 * block
    slots = rows // row_count * capacity
    full = width + (3 * experts + 127) // 128 * 128
    sizes = (width, row_count, capacity, block)
    line = Line()

    turned_shape = (step_count, top_count, row_count)
    own, = line(
        functools.partial(own_kernel, (width, row_count, experts)),
        "own",
        [((block, full), BF16)],
        [index],
        [],
        stored=[tokens, expert_ids.transpose(0, 2, 1), combine_weights.transpose(0, 2, 1)],
        scratch=[
            pltpu.VMEM(tokens.shape, BF16),
            pltpu.VMEM(turned_shape, jnp.int32),
            pltpu.VMEM(turned_shape, F32),
            pltpu.SemaphoreType.DMA((3,)),
        ],
    )
    later, _ = lax.optimization_barrier((shared_weights, own))
    shared_other = other_core(later)
    gather_groups, reduce_groups, order = (GATHER_GROUPS, REDUCE_GROUPS, ORDER) if planes == 4 else any_groups(planes)
    home = {k: (g, i, len(group)) for g, group in enumerate(gather_groups) for i, k in enumerate(group)}
    paired = any(1 in group and 3 in group for group in gather_groups)
    far = {0: own}
    for k in range(2, planes, 2):
        far[k] = across(own, k)
    if not paired:
        far[1] = across(own, 1)
    held = {}
    hop, wide, leaving, chosen, mine, back, got, rest, last, arrived, packed, kept, coming, crossed = ({} for _ in range(14))

    def load(name, weights):
        held[name], = line(
            load_kernel,
            "load",
            [(weights.shape, BF16)],
            [],
            [],
            stored=[weights],
            scratch=[pltpu.SemaphoreType.DMA((4,))],
        )

    def enter(g):
        group = gather_groups[g]
        if paired and 1 in group:
            near_far, = line(pack_kernel, "pack", [((2 * block, full), BF16)], [], [own, far[2]])
            packed[g] = across(near_far, 1)
            packed[g], = line(gate_kernel, "enter", [(packed[g].shape, BF16)], [], [packed[g]], alias={0: 0})
        elif len(group) > 1:
            packed[g], = line(
                pack_kernel, "pack", [((len(group) * block, full), BF16)], [], [far[k] for k in group]
            )
        elif group[0] > 0:
            k = group[0]
            packed[g], = line(gate_kernel, "enter", [((block, full), BF16)], [], [far[k]], alias={0: 0})
            far[k] = packed[g]
        else:
            packed[g] = own
        for k in group:
            if not paired and k >= 2 and k & 1 == 0:
                far[k + 1] = across(far[k], 1)
        hop[g] = first_hop(packed[g])

    def pack(g):
        count = 2 * len(gather_groups[g])
        packed[g], = line(pack_kernel, "pack", [((count * block, full), BF16)], [], [packed[g], hop[g]])
        wide[g] = second_hop(packed[g])

    def blocks(k):
        g, i, n = home[k]
        places = (i * block, (n + i) * block)
        return [packed[g], wide[g]], places * 2

    def dispatch(k):
        arrays, places = blocks(k)
        chosen[k], out = line(
            functools.partial(dispatch_kernel, (sizes, places)),
            "dispatch",
            [((slots, full), BF16)] * 2,
            [index],
            arrays,
        )
        leaving[k] = other_core(out)

    def expert(k):
        mine[k], out = line(
            functools.partial(expert_kernel, experts),
            "expert",
            [((slots, width), BF16)] * 2,
            [index],
            [chosen[k], leaving[k], held["gate"], held["up"], held["down"]],
            scratch=[pltpu.VMEM((2 * slots, full), BF16), pltpu.VMEM((2 * slots, units), BF16)],
        )
        back[k] = other_core(out)

    def shared():
        arrays, places = blocks(0)
        kept["shared"], held["up"] = line(
            functools.partial(shared_kernel, (sizes, places)),
            "shared",
            [((rows, width), F32), (w_up.shape, BF16)],
            [],
            [*arrays, shared_weights, shared_other],
            stored=[w_up],
            scratch=[pltpu.VMEM((rows, width), BF16), pltpu.SemaphoreType.DMA((4,))],
        )

    def combine(r):
        group = reduce_groups[r]
        arrays, all_places = [], []
        for k in group:
            pair, places = blocks(k)
            arrays += [*pair, mine[k], back[k]]
            all_places.append(places)
        shared_at = group.index(0) if 0 in group else -1
        if 0 in group:
            arrays.append(kept["shared"])
        half = 2 * block * len(group)
        kept[r], send = line(
            functools.partial(combine_kernel, (sizes, all_places, shared_at)),
            f"combine{len(group)}",
            [((half, width), F32), ((half, width), BF16)],
            [index],
            arrays,
        )
        got[r] = second_hop(send)

    def middle(r):
        group = reduce_groups[r]
        if group == (1,):
            out, = line(
                functools.partial(sum_kernel, [[(0, 0), (1, 0)]]),
                "sum",
                [((2 * block, width), BF16)],
                [],
                [kept[r], got[r]],
            )
            crossed[1] = across(out, 1)
            return
        half = block * len(group)
        rest[r], send = line(
            middle_kernel,
            "middle",
            [((half, width), F32), ((half, width), BF16)],
            [],
            [kept[r], got[r]] + ([crossed[1]] if 0 in group else []),
        )
        last[r] = first_hop(send)

    def leave(r):
        group = reduce_groups[r]
        for k in group:
            if k < 2:
                continue
            both = [k]
            arrays, pieces = [rest[r], last[r]], []
            for j in both:
                at = group.index(j) * block
                pieces.append([(0, at), (1, at)])
            if k >= 2 and k & 1 == 0 and not DIRECT:
                array, at = arrived.pop(k + 1)
                arrays.append(array)
                pieces[0].append((2, at))
            out, = line(
                functools.partial(sum_kernel, pieces), "leave", [((len(both) * block, width), BF16)], [], arrays
            )
            out = across(out, 1 if k & 1 and not DIRECT else k)
            for i, j in enumerate(both):
                arrived[j] = (out, i * block)
                coming[j] = out

    def final():
        r = [r for r, group in enumerate(reduce_groups) if 0 in group][0]
        at = reduce_groups[r].index(0) * block
        arrays, pieces = [rest[r], last[r]], [(0, at), (1, at)]
        for array, at in arrived.values():
            pieces.append((len(arrays), at))
            arrays.append(array)
        out, = line(
            functools.partial(sum_kernel, [pieces]),
            "final",
            [((step_count, row_count, width), BF16)],
            [],
            arrays,
            inside=False,
        )
        return out

    steps = {
        "E": enter,
        "K": pack,
        "L": lambda i: load("down", w_down) if i else load("gate", w_gate),
        "D": dispatch,
        "X": expert,
        "S": lambda i: shared(),
        "C": combine,
        "M": middle,
        "V": leave,
    }
    stores = {"h": hop, "w": wide, "c": leaving, "b": back, "g": got, "l": last, "a": coming, "z": crossed}
    for step in order:
        step, *also = step.split(":")
        line.also = [stores[name[0]][int(name[1:])] for name in also]
        steps[step[0]](int(step[1:]))
    return final()


def solution(mesh):
    placed = (
        P(None, AXIS, None),
        P(None, AXIS, None),
        P(None, AXIS, None),
        P(AXIS, None, None),
        P(AXIS, None, None),
        P(AXIS, None, None),
        P(None, None, AXIS),
    )
    return jax.shard_map(
        shards, mesh=mesh, in_specs=placed, out_specs=P(None, AXIS, None), check_vma=False
    )
```
